128 devices in a mesh: row: 16 (over x, z_hi, core), rep: 8 (over z_lo, y).
Axes of the slice: x: 4, y: 4, z: 4 (z_hi: 2, z_lo: 2; z = z_hi * 2 + z_lo), core: 2. Of those that a mesh axis runs over, the one named last changes fastest.
Arguments:
- features: bfloat16 [32768, 256], P('row'), may hold values from -6 to 6
- weight: bfloat16 [256, 256], replicated, may hold values from -0.375 to 0.375
- tile_values: bfloat16 [16, 8, 2, 192, 128, 128], P('row', 'rep'), may hold values from -0.0546875 to 0.0546875
- tile_rows: int32 [16, 8, 2, 192], P('row', 'rep'), may hold values from 0 to 15, as said below
- tile_cols: int32 [16, 8, 2, 192], P('row', 'rep'), may hold values from 0 to 15, as said below
- tile_count: int32 [16, 8, 2], P('row', 'rep'), may hold values from 24 to 192
- train_mask: int32 [32768], P(('row', 'rep')), may hold values 0 or 1
- upstream: bfloat16 [32768, 256], P(('row', 'rep')), may hold values from -24 to 24
Outputs:
- activated: bfloat16 [32768, 256], P(('row', 'rep'))
- weight_grad: float32 [256, 256], replicated
- feature_grad: bfloat16 [32768, 256], P(('row', 'rep'))
The draws below stay inside these ranges and needn't reach their ends.
Inputs may be any that keep to these rules, and one draw needn't show every extreme that they name: Within one list of 192 slots no pair (tile_rows, tile_cols) repeats. `tile_cols`: paired slot by slot with tile_rows.
All inputs are finite; a program needn't handle non-finite values. No bound on the sum of `train_mask` on one device may be relied on, other than what follows from the above.
Results may differ from the reference program's by a relative error of at most 0.025.
Values may be sent and summed in bfloat16 or wider, within the bound.
No kernel may reach another device: no remote copies, remote signals or barrier semaphores. Data moves between devices by JAX's collectives and lax.ppermute only.
A program may use at most 128 MiB of HBM per device.

```python
import math
import jax
import jax.numpy as jnp
from jax import lax

F = 256
TILE = 128
TB = 16
KMAX = 192
S_REP = 2
NODES = 32768
N_ROW = 16
N_REP = 8


def tile_layout(key):
    layout_key = jax.random.fold_in(key, 11)
    lists = N_ROW * N_REP * S_REP
    keys = jax.random.split(layout_key, lists)
    chosen = jax.vmap(lambda list_key: jax.random.permutation(list_key, TB * TB)[:KMAX])(keys)
    return chosen.reshape(N_ROW, N_REP, S_REP, KMAX).astype(jnp.int32)


def draw_tile_rows(key, part):
    return tile_layout(key) // TB


def draw_tile_cols(key, part):
    return tile_layout(key) % TB


def draw_tile_count(key, part):
    key = jax.random.fold_in(key, 23)
    level_key, spot_key = jax.random.split(key)
    lists = N_ROW * N_REP * S_REP
    levels = jax.random.randint(level_key, (lists,), 0, 4).astype(jnp.int32)
    counts = jnp.int32(KMAX) // jnp.left_shift(jnp.int32(1), levels)
    spot = jax.random.randint(spot_key, (), 0, lists).astype(jnp.int32)
    counts = jnp.where(jnp.arange(lists, dtype=jnp.int32) == spot, jnp.int32(KMAX), counts)
    return counts.reshape(N_ROW, N_REP, S_REP).astype(jnp.int32)


def set_ends(entries, stream_key, least, high):
    longest = entries.shape.index(max(entries.shape))
    spots = []
    for shift in (0, 1):
        where = [jax.random.randint(jax.random.fold_in(stream_key, axis), (), 0, length) for axis, length in enumerate(entries.shape)]
        where[longest] = (where[longest] + shift) % entries.shape[longest]
        spots.append(tuple(where))
    return entries.at[spots[0]].set(least).at[spots[1]].set(high)


def raised(values, rng, source, target, blocks, factor):
    def block_of(position):
        return (jnp.arange(values.shape[position]) // (values.shape[position] // blocks)).reshape((-1,) + (1,) * (values.ndim - 1 - position))

    near = jax.random.permutation(rng, blocks)[block_of(target)]
    other_side = (block_of(target) + blocks // 2) % blocks
    return jnp.where((block_of(source) == near) | (block_of(source) == other_side), factor * values, values)


def block_levels(stream_key, shape, cuts, least, high):
    factor_of, own = 1.0, jax.random.fold_in(stream_key, 6)
    for axis_at, blocks in cuts:
        heights = jnp.exp(jax.random.uniform(jax.random.fold_in(own, axis_at), (blocks,), jnp.float32, least / len(cuts), high / len(cuts)))
        factor_of = factor_of * jnp.repeat(heights, shape[axis_at] // blocks).reshape([-1 if axis == axis_at else 1 for axis in range(len(shape))])
    return factor_of


def scatter_about(key, shape, scale, bound, cuts=(), kind=jnp.bfloat16):
    drawn = scale * jax.random.normal(key, shape, jnp.float32)
    if cuts:
        drawn = drawn * block_levels(key, shape, cuts, -0.22, 0.18)
    return jnp.clip(drawn, -bound, bound).astype(kind)


def heavy_noise(own_key, shape, width, most, cuts, heavy, held_as=jnp.bfloat16):
    values = width * jax.random.normal(own_key, shape, jnp.float32)
    if cuts:
        values = values * block_levels(own_key, shape, cuts, -0.22, 0.18)
    return jnp.clip(raised(values, jax.random.fold_in(own_key, 3), *heavy), -most, most).astype(held_as)


def setup_inputs(seed: int = 0) -> dict:
    key_of = jax.random.split(jax.random.key(seed), 9)
    features = scatter_about(key_of[0], (NODES, F), 1.0, 6.0, ((0, 16),))
    weight = scatter_about(key_of[1], (F, F), F ** -0.5, 0.375)
    tile_values = scatter_about(key_of[2], (N_ROW, N_REP, S_REP, KMAX, TILE, TILE), (N_ROW * KMAX * TILE // (2 * TB)) ** -0.5, 0.0546875, ((0, 16), (1, 8)))
    tile_rows = draw_tile_rows(jax.random.fold_in(key_of[8], 71), 0)
    tile_cols = draw_tile_cols(jax.random.fold_in(key_of[8], 71), 0)
    tile_count = draw_tile_count(jax.random.fold_in(key_of[8], 71), 0)
    train_mask = set_ends((jax.random.randint(key_of[6], (NODES,), 0, 4) < 1).astype(jnp.int32), jax.random.fold_in(key_of[6], 1), 0, 1)
    upstream = heavy_noise(key_of[7], (NODES, F), 1.0, 24.0, ((0, 128),), (0, 1, 128, 5.5))
    return dict(features=features, weight=weight, tile_values=tile_values, tile_rows=tile_rows, tile_cols=tile_cols, tile_count=tile_count, train_mask=train_mask, upstream=upstream)


def tile_product(tile_block, source, gather_index, place_index, count, transpose):
    pieces = source.reshape(TB, TILE, F)[gather_index]
    form = 'kba,kbf->kaf' if transpose else 'kab,kbf->kaf'
    product = jnp.einsum(form, tile_block.astype(jnp.float32), pieces.astype(jnp.float32))
    live = jnp.arange(KMAX, dtype=jnp.int32) < count
    hits = (place_index[None, :] == jnp.arange(TB, dtype=jnp.int32)[:, None]) & live[None, :]
    selector = jnp.where(hits, 1.0, 0.0).astype(jnp.float32)
    placed = jnp.dot(selector, product.reshape(KMAX, TILE * F), precision=lax.Precision.HIGHEST)
    return placed.reshape(TB * TILE, F)

def reference(features, weight, tile_values, tile_rows, tile_cols, tile_count, train_mask, upstream):
    block_rows = TB * TILE
    lists = N_ROW * N_REP * S_REP
    flat_values = tile_values.reshape(lists, KMAX, TILE, TILE)
    flat_rows = tile_rows.reshape(lists, KMAX)
    flat_cols = tile_cols.reshape(lists, KMAX)
    flat_count = tile_count.reshape(lists)
    blocks = features.reshape(N_ROW, block_rows, F)

    def locate(list_index):
        block = list_index // (N_REP * S_REP)
        rest = list_index % (N_REP * S_REP)
        replica = rest // S_REP
        section = rest % S_REP
        source = (block - replica * S_REP - section) % N_ROW
        return (block, source)

    def forward_step(list_index, total):
        block, source = locate(list_index)
        term = tile_product(flat_values[list_index], blocks[source], flat_cols[list_index], flat_rows[list_index], flat_count[list_index], False)
        return total.at[block].add(term)
    total = lax.fori_loop(0, lists, forward_step, jnp.zeros((N_ROW, block_rows, F), jnp.float32))
    aggregate = total.reshape(NODES, F).astype(jnp.bfloat16)
    logits = jnp.dot(aggregate, weight, preferred_element_type=jnp.float32)
    sigmoid_part = jax.nn.sigmoid(logits)
    activated = (logits * sigmoid_part).astype(jnp.bfloat16)
    slope = sigmoid_part * (1.0 + logits * (1.0 - sigmoid_part))
    masked = (upstream.astype(jnp.float32) * train_mask.astype(jnp.float32)[:, None] * slope).astype(jnp.bfloat16)
    weight_grad = jnp.dot(aggregate.T, masked, preferred_element_type=jnp.float32) * (1.0 / math.sqrt(NODES))
    back = jnp.dot(masked, weight.T, preferred_element_type=jnp.float32).astype(jnp.bfloat16)
    back_blocks = back.reshape(N_ROW, block_rows, F)

    def backward_step(list_index, total_grad):
        block, source = locate(list_index)
        term = tile_product(flat_values[list_index], back_blocks[block], flat_rows[list_index], flat_cols[list_index], flat_count[list_index], True)
        return total_grad.at[source].add(term)
    total_grad = lax.fori_loop(0, lists, backward_step, jnp.zeros((N_ROW, block_rows, F), jnp.float32))
    feature_grad = total_grad.reshape(NODES, F).astype(jnp.bfloat16)
    return (activated, weight_grad, feature_grad)
```

```python
import functools
import math

import jax
import jax.numpy as jnp
from jax import lax
from jax.experimental import pallas as pl
from jax.experimental.pallas import tpu as pltpu
from jax.sharding import PartitionSpec as P

TB = 16
TILE = 128
CHUNK = 48
VMEM = pl.BlockSpec(memory_space=pltpu.VMEM)
SMEM = pl.BlockSpec(memory_space=pltpu.SMEM)
NT = (((1,), (1,)), ((), ()))
TN = (((0,), (0,)), ((), ()))


def params(mib, **more):
    return pltpu.CompilerParams(vmem_limit_bytes=mib << 20, **more)


def in_vmem(array):
    return pltpu.with_memory_space_constraint(array, pltpu.VMEM)


def build_kernel(rows, cols, count, tiles, panels):
    part, chunk = pl.program_id(0), pl.program_id(1)

    @pl.when(chunk == 0)
    def _():
        def clear(b, carry):
            panels[part, b] = jnp.zeros(panels.shape[2:], panels.dtype)
            return carry

        lax.fori_loop(0, TB, clear, 0)

    def place(t, carry):
        slot = chunk * CHUNK + t
        row = pl.multiple_of(rows[part, slot] * TILE, TILE)
        panels[part, cols[part, slot], pl.ds(row, TILE), :] = tiles[0, t]
        return carry

    lax.fori_loop(0, jnp.clip(count[part] - chunk * CHUNK, 0, CHUNK), place, 0)


def build(tile_values, tile_rows, tile_cols, tile_count):
    sections, slots = tile_rows.shape

    def block(part, chunk, rows, cols, count):
        last = lax.div(count[part] - 1, CHUNK)
        return part, jnp.minimum(chunk, last), 0, 0

    return pl.pallas_call(
        build_kernel,
        grid_spec=pltpu.PrefetchScalarGridSpec(
            num_scalar_prefetch=3,
            grid=(sections, slots // CHUNK),
            in_specs=[pl.BlockSpec((1, CHUNK, TILE, TILE), block)],
            out_specs=VMEM,
        ),
        out_shape=pltpu.VMEM((sections, TB, TB * TILE, TILE), jnp.bfloat16),
        compiler_params=params(12),
        cost_estimate=pl.CostEstimate(flops=0, bytes_accessed=30 << 20, transcendentals=0),
        name="build",
    )(tile_rows, tile_cols, tile_count, tile_values)


def wide(panels, part, rows):
    return jnp.concatenate([panels[part, b, rows, :] for b in range(TB)], axis=1)


def forward_kernel(share, mine, panels, first, second, *outs):
    for d, out in enumerate(outs):
        q = lax.rem(mine[0] + d, len(outs))
        rows = pl.ds(pl.multiple_of(q * share, share), share)
        total = jnp.dot(wide(panels, 0, rows), first[...], preferred_element_type=jnp.float32)
        total += jnp.dot(wide(panels, 1, rows), second[...], preferred_element_type=jnp.float32)
        out[...] = total.astype(out.dtype)


def forward(mine, panels, first, second, shares):
    rows, width = first.shape
    share = rows // shares
    return pl.pallas_call(
        functools.partial(forward_kernel, share),
        in_specs=[SMEM, VMEM, VMEM, VMEM],
        out_specs=[VMEM] * shares,
        out_shape=[jax.ShapeDtypeStruct((share, width), jnp.bfloat16)] * shares,
        compiler_params=params(20),
        cost_estimate=pl.CostEstimate(flops=4 * rows * rows * width, bytes_accessed=4 << 20, transcendentals=0),
        name="forward",
    )(mine, in_vmem(panels), first, second)


def middle_kernel(shares, mine, *refs):
    parts = refs[:shares]
    weight, cotangent, activated, back, term = refs[shares : shares + 5]
    sends = refs[shares + 5 :]
    total = parts[0][...].astype(jnp.float32)
    for part in parts[1:]:
        total += part[...].astype(jnp.float32)
    aggregate = total.astype(jnp.bfloat16)
    logits = jnp.dot(aggregate, weight[...], preferred_element_type=jnp.float32)
    sigmoid_part = jax.nn.sigmoid(logits)
    activated[...] = (logits * sigmoid_part).astype(jnp.bfloat16)
    slope = sigmoid_part * (1.0 + logits * (1.0 - sigmoid_part))
    masked = (cotangent[...] * slope).astype(jnp.bfloat16)
    term[...] = lax.dot_general(aggregate, masked, TN, preferred_element_type=jnp.float32)
    turned = lax.dot_general(weight[...], masked, NT, preferred_element_type=jnp.float32)
    turned = turned.astype(jnp.bfloat16)
    back[...] = turned
    width = weight.shape[0]
    some = width // shares
    for d, send in enumerate(sends, 1):
        q = lax.rem(mine[0] + d, shares)
        send[:width, :] = turned
        send[width:, :] = term[pl.ds(pl.multiple_of(q * some, some), some), :].astype(jnp.bfloat16)


def middle(mine, parts, weight, cotangent):
    shares = len(parts)
    share, width = cotangent.shape
    bf16, f32 = jnp.bfloat16, jnp.float32
    result = pl.pallas_call(
        functools.partial(middle_kernel, shares),
        in_specs=[SMEM] + [VMEM] * (shares + 2),
        out_specs=[VMEM] * (shares + 2),
        out_shape=[
            jax.ShapeDtypeStruct((share, width), bf16),
            jax.ShapeDtypeStruct((width, share), bf16),
            jax.ShapeDtypeStruct((width, width), f32),
        ]
        + [jax.ShapeDtypeStruct((width + width // shares, share), bf16)] * (shares - 1),
        compiler_params=params(12),
        name="middle",
    )(mine, *parts, weight, cotangent)
    return result[0], result[1], result[2], result[3:]


def backward_kernel(part, share, rotate, mine, panels, *refs):
    backs, out = refs[:-1], refs[-1]
    shares = len(backs)
    width = backs[0].shape[1]
    for d in range(out.shape[0]):
        q = lax.rem(mine[0] + d, shares) if rotate else d
        total = None
        for e, back in enumerate(backs):
            p = lax.rem(mine[0] + shares - e, shares)
            rows = pl.ds(pl.multiple_of(p * share, share), share)
            block = jnp.concatenate([panels[part, 2 * q + h, rows, :] for h in range(2)], axis=1)
            product = jnp.dot(back[:width, :], block, preferred_element_type=jnp.float32)
            total = product if total is None else total + product
        out[d] = total.astype(out.dtype)


def backward(part, rotate, mine, panels, backs, dtype):
    shares = len(backs)
    width = share = backs[0].shape[1]
    return pl.pallas_call(
        functools.partial(backward_kernel, part, share, rotate),
        in_specs=[SMEM] + [VMEM] * (shares + 1),
        out_specs=VMEM,
        out_shape=jax.ShapeDtypeStruct((shares, width, share), dtype),
        compiler_params=params(12),
        cost_estimate=pl.CostEstimate(flops=2 * (shares * share) ** 2 * width, bytes_accessed=3 << 20, transcendentals=0),
        name="backward",
    )(mine, in_vmem(panels), *backs)


def merge_kernel(mine, own, other, *outs):
    for d, out in enumerate(outs):
        q = lax.rem(mine[0] + d, len(outs))
        out[...] = (own[d] + other[q].astype(jnp.float32)).astype(out.dtype)


def merge(mine, own, other):
    shares, width, share = own.shape
    return pl.pallas_call(
        merge_kernel,
        in_specs=[SMEM, VMEM, VMEM],
        out_specs=[VMEM] * shares,
        out_shape=[jax.ShapeDtypeStruct((width, share), jnp.bfloat16)] * shares,
        compiler_params=params(12),
        name="merge",
    )(mine, own, other)


def finish_kernel(*refs):
    total = refs[0][...].astype(jnp.float32)
    for part in refs[1:-1]:
        total += part[...].astype(jnp.float32)
    refs[-1][...] = total.T.astype(jnp.bfloat16)


def finish(parts):
    width, share = parts[0].shape
    return pl.pallas_call(
        finish_kernel,
        in_specs=[VMEM] * len(parts),
        out_specs=VMEM,
        out_shape=jax.ShapeDtypeStruct((share, width), jnp.bfloat16),
        compiler_params=params(12),
        name="finish",
    )(*parts)


def pairs(row_devices, rep_devices, target):
    found = []
    for i in range(row_devices):
        for r in range(rep_devices):
            j, q = target(i, r)
            found.append((i * rep_devices + r, (j % row_devices) * rep_devices + q % rep_devices))
    return found


def per_device(features, weight, tile_values, tile_rows, tile_cols, tile_count, train_mask, upstream):
    rows_n, reps = lax.axis_size("row"), lax.axis_size("rep")
    sections = rows_n // reps
    mine = lax.axis_index("rep").astype(jnp.int32).reshape(1)

    def moved(value, target):
        return lax.ppermute(value, ("row", "rep"), pairs(rows_n, reps, target))

    first = moved(features, lambda j, r: (j + sections * r, r))
    panels = build(tile_values[0, 0], tile_rows[0, 0], tile_cols[0, 0], tile_count[0, 0])
    second = moved(first, lambda i, r: (i - 1, r - 1) if i % 2 else (i + 1, r))
    cotangent = upstream.astype(jnp.float32) * train_mask.astype(jnp.float32)[:, None]

    partial_rows = forward(mine, panels, first, second, reps)
    received = [partial_rows[0]] + [
        moved(partial_rows[d], lambda i, r, d=d: (i, r + d)) for d in range(1, reps)
    ]
    activated, back, term, sends = middle(mine, received, weight, cotangent)

    arrived = [moved(send, lambda i, r, d=d: (i, r + d)) for d, send in enumerate(sends, 1)]
    backs = [back] + arrived
    late = backward(1, False, mine, panels, backs, jnp.bfloat16)
    late = moved(late, lambda i, r: (i - 1, r) if i % 2 else (i + 1, r + 1))
    early = backward(0, True, mine, panels, backs, jnp.float32)
    merged = merge(mine, early, late)
    homes = [
        moved(piece, lambda i, r, d=d: (i - sections * r, r + d)) for d, piece in enumerate(merged)
    ]
    feature_grad = finish(homes)

    width = weight.shape[0]
    some = width // reps
    strip = lax.dynamic_slice_in_dim(term, mine[0] * some, some, 0)
    for piece in arrived:
        strip = strip + piece[width:].astype(jnp.float32)
    bit = 1
    while bit < rows_n:
        strip = strip + moved(strip, lambda i, r, bit=bit: (i ^ bit, r))
        bit *= 2
    scale = 1.0 / math.sqrt(features.shape[0] * rows_n)
    whole = strip * scale
    bit = 1
    while bit < reps:
        other = moved(whole, lambda i, r, bit=bit: (i, r ^ bit))
        upper = (mine[0] & bit) != 0
        whole = jnp.where(upper, jnp.concatenate([other, whole], 0), jnp.concatenate([whole, other], 0))
        bit *= 2
    return activated, whole, feature_grad


def solution(mesh):
    placed = (
        P("row", None),
        P(),
        P("row", "rep", None, None, None, None),
        P("row", "rep", None, None),
        P("row", "rep", None, None),
        P("row", "rep", None),
        P(("row", "rep")),
        P(("row", "rep"), None),
    )
    return jax.shard_map(
        per_device,
        mesh=mesh,
        in_specs=placed,
        out_specs=(P(("row", "rep"), None), P(), P(("row", "rep"), None)),
        check_vma=False,
    )
```

```python
import functools
import math

import jax
import jax.numpy as jnp
from jax import lax
from jax.experimental import pallas as pl
from jax.experimental.pallas import tpu as pltpu
from jax.sharding import PartitionSpec as P

TB = 16
TILE = 128
CHUNK = 48
VMEM = pl.BlockSpec(memory_space=pltpu.VMEM)
SMEM = pl.BlockSpec(memory_space=pltpu.SMEM)
NT = (((1,), (1,)), ((), ()))
TN = (((0,), (0,)), ((), ()))


def params(mib, **more):
    return pltpu.CompilerParams(vmem_limit_bytes=mib << 20, **more)


def in_vmem(array):
    return pltpu.with_memory_space_constraint(array, pltpu.VMEM)


def build_kernel(part, rows, cols, count, tiles, *refs):
    panels, token = refs[-2:]
    chunk = pl.program_id(0)
    token[...] = jnp.zeros(token.shape, token.dtype)

    @pl.when(chunk == 0)
    def _():
        def clear(b, carry):
            panels[part, b] = jnp.zeros(panels.shape[2:], panels.dtype)
            return carry

        lax.fori_loop(0, TB, clear, 0)

    def place(t, carry):
        slot = chunk * CHUNK + t
        row = pl.multiple_of(rows[part, slot] * TILE, TILE)
        panels[part, cols[part, slot], pl.ds(row, TILE), :] = tiles[0, t]
        return carry

    lax.fori_loop(0, jnp.clip(count[part] - chunk * CHUNK, 0, CHUNK), place, 0)


def build(part, tile_values, tile_rows, tile_cols, tile_count, *more):
    sections, slots = tile_rows.shape

    def block(chunk, rows, cols, count):
        last = lax.div(count[part] - 1, CHUNK)
        return part, jnp.minimum(chunk, last), 0, 0

    return pl.pallas_call(
        functools.partial(build_kernel, part),
        grid_spec=pltpu.PrefetchScalarGridSpec(
            num_scalar_prefetch=3,
            grid=(slots // CHUNK,),
            in_specs=[pl.BlockSpec((1, CHUNK, TILE, TILE), block)] + [VMEM] * len(more),
            out_specs=[VMEM, VMEM],
        ),
        out_shape=[
            pltpu.VMEM((sections, TB, TB * TILE, TILE), jnp.bfloat16),
            jax.ShapeDtypeStruct((8, 128), jnp.int32),
        ],
        input_output_aliases={4: 0} if more else {},
        compiler_params=params(12),
        cost_estimate=pl.CostEstimate(flops=0, bytes_accessed=15 << 20, transcendentals=0),
        name="build",
    )(tile_rows, tile_cols, tile_count, pltpu.with_memory_space_constraint(tile_values, pltpu.HBM), *map(in_vmem, more[:1]), *more[1:])


def place_of():
    return lax.axis_index("rep"), lax.rem(lax.axis_index("row"), 2)


def with_panels(kernel, name, panels, operands, outs, mib, flops=0):
    result = pl.pallas_call(
        kernel,
        in_specs=[VMEM] * (1 + len(operands)),
        out_specs=[VMEM] * (1 + len(outs)),
        out_shape=[pltpu.VMEM(panels.shape, panels.dtype), *outs],
        input_output_aliases={0: 0},
        compiler_params=params(mib),
        cost_estimate=pl.CostEstimate(flops=flops, bytes_accessed=2 << 20, transcendentals=0),
        name=name,
    )(in_vmem(panels), *operands)
    return result[0], result[1:]


def wide(panels, part, rows, at, size):
    return jnp.concatenate([panels[part, at + b, rows, :] for b in range(size)], axis=1)


def first_kernel(share, panels, source, token, same, out):
    replica, _ = place_of()
    for d in range(out.shape[0]):
        q = lax.rem(replica + d, out.shape[0])
        rows = pl.ds(pl.multiple_of(q * share, share), share)
        out[d] = jnp.dot(wide(panels, 0, rows, 0, TB), source[...], preferred_element_type=jnp.float32)


def second_kernel(share, shares, ds, panels, carried, inner, other, same, *outs):
    replica, core = place_of()
    source = jnp.where(core == 1, inner[...], other[...])
    for d, out in zip(ds, outs):
        q = lax.rem(replica + d, shares)
        rows = pl.ds(pl.multiple_of(q * share, share), share)
        total = carried[d] + jnp.dot(wide(panels, 1, rows, 0, TB), source, preferred_element_type=jnp.float32)
        out[...] = total.astype(out.dtype)


def middle_kernel(shares, panels, *refs):
    parts = refs[:shares]
    weight, upstream, train_mask, same, activated, back, term, *sends = refs[shares:]
    replica, _ = place_of()
    total = parts[0][...].astype(jnp.float32)
    for part in parts[1:]:
        total += part[...].astype(jnp.float32)
    aggregate = total.astype(jnp.bfloat16)
    logits = jnp.dot(aggregate, weight[...], preferred_element_type=jnp.float32)
    sigmoid_part = jax.nn.sigmoid(logits)
    activated[...] = (logits * sigmoid_part).astype(jnp.bfloat16)
    slope = sigmoid_part * (1.0 + logits * (1.0 - sigmoid_part))
    trained = jnp.broadcast_to(train_mask[...].astype(jnp.float32), logits.shape[::-1]).T
    masked = (upstream[...].astype(jnp.float32) * trained * slope).astype(jnp.bfloat16)
    turned = lax.dot_general(weight[...], masked, NT, preferred_element_type=jnp.float32).astype(jnp.bfloat16)
    back[...] = turned
    term[...] = lax.dot_general(aggregate, masked, TN, preferred_element_type=jnp.float32)
    width = weight.shape[0]
    some = width // shares
    for d, send in enumerate(sends, 1):
        at = pl.multiple_of(lax.rem(replica + d, shares) * some, some)
        send[:width, :] = turned
        send[width:, :] = term[pl.ds(at, some), :].astype(jnp.bfloat16)


def product_of(panels, part, q, es, backs, shares):
    replica, _ = place_of()
    width = share = backs[0].shape[1]
    total = None
    for e, back in zip(es, backs):
        p = lax.rem(replica + shares - e, shares)
        rows = pl.ds(pl.multiple_of(p * share, share), share)
        product = jnp.dot(back[:width, :], wide(panels, part, rows, 2 * q, 2), preferred_element_type=jnp.float32)
        total = product if total is None else total + product
    return total


def heads_kernel(shares, es, panels, *refs):
    backs = refs[: len(es)]
    same, late, early = refs[len(es) :]
    for part, out in ((1, late), (0, early)):
        for q in range(shares):
            out[q] = product_of(panels, part, q, es, backs, shares)


def tails_kernel(part, shares, es, qs, panels, carried, *refs):
    backs = refs[: len(es)]
    same, out = refs[len(es) :]
    for n, q in enumerate(qs):
        out[n] = (carried[q] + product_of(panels, part, q, es, backs, shares)).astype(out.dtype)


def tails_strip_kernel(part, shares, es, qs, panels, carried, *refs):
    backs, (term, *pieces) = refs[: len(es)], refs[len(es) : len(es) + 4]
    same, out, strips = refs[len(es) + 4 :]
    tails_kernel(part, shares, es, qs, panels, carried, *backs, same, out)
    replica, _ = place_of()
    width = term.shape[0]
    some = width // shares
    total = term[pl.ds(pl.multiple_of(replica * some, some), some), :]
    for piece in [*pieces, *backs]:
        total += piece[width:, :].astype(jnp.float32)
    for n in range(strips.shape[0]):
        strips[n] = total.astype(strips.dtype)


def merge_kernel(own, first, second, strips, *outs):
    replica, _ = place_of()
    half, width, _ = first.shape
    strip = strips[0].astype(jnp.float32)
    for n in range(1, strips.shape[0]):
        strip += strips[n].astype(jnp.float32)
    strip = strip.astype(jnp.bfloat16)
    for d, out in enumerate(outs):
        q = lax.rem(replica + d, len(outs))
        n = lax.rem(q, half)
        late = jnp.where(q < half, first[n], second[n])
        out[:width, :] = (own[q] + late.astype(jnp.float32)).astype(out.dtype)
        out[width:, :] = strip


def merge(own, first, second, strips):
    shares, width, share = own.shape
    return pl.pallas_call(
        merge_kernel,
        in_specs=[VMEM] * 4,
        out_specs=[VMEM] * shares,
        out_shape=[jax.ShapeDtypeStruct((width + strips.shape[1], share), jnp.bfloat16)] * shares,
        compiler_params=params(12),
        name="merge",
    )(own, first, second, strips)


def finish_kernel(scale, *refs):
    got, (home, whole) = refs[:-2], refs[-2:]
    replica, _ = place_of()
    width = whole.shape[0]
    some = width // len(got)
    total = got[0][:width, :].astype(jnp.float32)
    for part in got[1:]:
        total += part[:width, :].astype(jnp.float32)
    home[...] = total.T.astype(home.dtype)
    for d, part in enumerate(got):
        at = pl.multiple_of(lax.rem(replica + len(got) - d, len(got)) * some, some)
        whole[pl.ds(at, some), :] = part[width:, :].astype(jnp.float32) * scale


def finish(scale, width, got):
    share = got[0].shape[1]
    return pl.pallas_call(
        functools.partial(finish_kernel, scale),
        in_specs=[VMEM] * len(got),
        out_specs=[VMEM, VMEM],
        out_shape=[
            jax.ShapeDtypeStruct((share, width), jnp.bfloat16),
            jax.ShapeDtypeStruct((width, share), jnp.float32),
        ],
        compiler_params=params(12),
        name="finish",
    )(*got)


def pairs(row_devices, rep_devices, target):
    found = []
    for i in range(row_devices):
        for r in range(rep_devices):
            j, q = target(i, r)
            found.append((i * rep_devices + r, (j % row_devices) * rep_devices + q % rep_devices))
    return found


MAIN_FROM = (0, 5, 2, 4, 7, 1, 6, 3)
OTHER_FROM = (1, 6, 3, 0, 5, 2, 4, 7)


def per_device(features, weight, tile_values, tile_rows, tile_cols, tile_count, train_mask, upstream):
    rows_n, reps = lax.axis_size("row"), lax.axis_size("rep")
    sections = rows_n // reps
    width = weight.shape[0]
    share = features.shape[0] // reps
    bf16, f32 = jnp.bfloat16, jnp.float32

    def moved(value, target):
        return lax.ppermute(value, ("row", "rep"), pairs(rows_n, reps, target))

    def fetched(value, back, sources, wanted=lambda i: True):
        found = [
            (((i - sections * r - back) % rows_n) * reps + sources[r], i * reps + r)
            for i in range(rows_n)
            for r in range(reps)
            if wanted(i)
        ]
        return lax.ppermute(value, ("row", "rep"), found)

    def to_other_core(value):
        return lax.ppermute(value, ("row", "rep"), [((i - 1) * reps + r, i * reps + r) for i in range(1, rows_n, 2) for r in range(reps)])

    main = fetched(features, 0, MAIN_FROM)
    lists = tile_values[0, 0], tile_rows[0, 0], tile_cols[0, 0], tile_count[0, 0]
    panels, token = build(0, *lists)
    held, token = lax.optimization_barrier((features, token))
    other = fetched(held, 1, OTHER_FROM, lambda i: i % 2 == 0)
    panels, token = build(1, *lists, panels, token)
    main, token = lax.optimization_barrier((main, token))
    inner = to_other_core(main)

    flops = features.shape[0] ** 2 * 2 * width
    panels, (carried,) = with_panels(
        functools.partial(first_kernel, share), "first", panels, [main, token],
        [jax.ShapeDtypeStruct((reps, share, width), f32)], 12, flops,
    )
    shares_out = {}
    for ds in ((1, 2, 3, 4), (5, 6, 7, 0)):
        panels, outs = with_panels(
            functools.partial(second_kernel, share, reps, ds), "second", panels, [carried, inner, other],
            [jax.ShapeDtypeStruct((share, width), bf16)] * len(ds), 12, flops // 2,
        )
        shares_out.update(zip(ds, outs))
    received = [shares_out[0]] + [moved(shares_out[d], lambda i, r, d=d: (i, r + d)) for d in range(1, reps)]

    panels, results = with_panels(
        functools.partial(middle_kernel, reps), "middle", panels, [*received, weight, upstream, train_mask.reshape(1, share)],
        [
            jax.ShapeDtypeStruct((share, width), bf16),
            jax.ShapeDtypeStruct((width, share), bf16),
            jax.ShapeDtypeStruct((width, width), f32),
        ]
        + [jax.ShapeDtypeStruct((width + width // reps, share), bf16)] * (reps - 1),
        12,
    )
    activated, back, term, *sends = results
    backs = [back] + [moved(send, lambda i, r, d=d: (i, r + d)) for d, send in enumerate(sends, 1)]

    shares = tuple(range(reps))
    head, tail = shares[:4], shares[4:]
    halves = shares[: reps // 2], shares[reps // 2 :]
    sums = jax.ShapeDtypeStruct((reps, width, share), f32)
    panels, (late_sum, early_sum) = with_panels(
        functools.partial(heads_kernel, reps, head), "heads", panels, backs[:4], [sums, sums], 12, flops
    )
    piece_out = pltpu.VMEM((reps // 2, width, share), bf16)
    strip_out = jax.ShapeDtypeStruct((rows_n // 2, width // reps, width), bf16)
    panels, (piece, strips) = with_panels(
        functools.partial(tails_strip_kernel, 1, reps, tail, halves[0]), "late_strip", panels,
        [late_sum, *backs[4:], term, *backs[1:4]], [piece_out, strip_out], 12, flops // 4,
    )
    first = moved(piece, lambda i, r: (i - 1, r) if i % 2 else (i + 1, r + 1))
    panels, (piece,) = with_panels(
        functools.partial(tails_kernel, 1, reps, tail, halves[1]), "late", panels, [late_sum, *backs[4:]], [piece_out], 12, flops // 4
    )
    second = moved(piece, lambda i, r: (i - 1, r))
    panels, (own,) = with_panels(
        functools.partial(tails_kernel, 0, reps, tail, shares), "early", panels, [early_sum, *backs[4:]], [sums], 12, flops // 2
    )
    strips, own = lax.optimization_barrier((strips, own))
    same_core = [[i * reps + r for i in range(c, rows_n, 2)] for c in range(2) for r in range(reps)]
    strips = lax.all_to_all(strips + moved(strips, lambda i, r: (i ^ 1, r)), ("row", "rep"), 0, 0, axis_index_groups=same_core)

    merged = merge(own, first, second, strips)
    got = [moved(merged[d], lambda i, r, d=d: (i - sections * r, r + d)) for d in shares]
    feature_grad, whole = finish(1.0 / math.sqrt(features.shape[0] * rows_n), width, got)
    return activated, whole, feature_grad


def solution(mesh):
    placed = (
        P("row", None),
        P(),
        P("row", "rep", None, None, None, None),
        P("row", "rep", None, None),
        P("row", "rep", None, None),
        P("row", "rep", None),
        P(("row", "rep")),
        P(("row", "rep"), None),
    )
    return jax.shard_map(
        per_device,
        mesh=mesh,
        in_specs=placed,
        out_specs=(P(("row", "rep"), None), P(), P(("row", "rep"), None)),
        check_vma=False,
    )
```

```python
import functools
import math

import jax
import jax.numpy as jnp
from jax import lax
from jax.experimental import pallas as pl
from jax.experimental.pallas import tpu as pltpu
from jax.sharding import PartitionSpec as P

TB = 16
TILE = 128
CHUNK = 48
VMEM = pl.BlockSpec(memory_space=pltpu.VMEM)
SMEM = pl.BlockSpec(memory_space=pltpu.SMEM)
NT = (((1,), (1,)), ((), ()))
TN = (((0,), (0,)), ((), ()))


def params(mib, **more):
    return pltpu.CompilerParams(vmem_limit_bytes=mib << 20, **more)


def in_vmem(array):
    return pltpu.with_memory_space_constraint(array, pltpu.VMEM)


def build_kernel(part, rows, cols, count, tiles, *refs):
    panels, token = refs[-2:]
    chunk = pl.program_id(0)
    token[...] = jnp.zeros(token.shape, token.dtype)

    @pl.when(chunk == 0)
    def _():
        def clear(b, carry):
            panels[part, b] = jnp.zeros(panels.shape[2:], panels.dtype)
            return carry

        lax.fori_loop(0, TB, clear, 0)

    def place(t, carry):
        slot = chunk * CHUNK + t
        row = pl.multiple_of(rows[part, slot] * TILE, TILE)
        panels[part, cols[part, slot], pl.ds(row, TILE), :] = tiles[0, t]
        return carry

    lax.fori_loop(0, jnp.clip(count[part] - chunk * CHUNK, 0, CHUNK), place, 0)


def build(part, tile_values, tile_rows, tile_cols, tile_count, *more):
    sections, slots = tile_rows.shape

    def block(chunk, rows, cols, count):
        last = lax.div(count[part] - 1, CHUNK)
        return part, jnp.minimum(chunk, last), 0, 0

    return pl.pallas_call(
        functools.partial(build_kernel, part),
        grid_spec=pltpu.PrefetchScalarGridSpec(
            num_scalar_prefetch=3,
            grid=(slots // CHUNK,),
            in_specs=[pl.BlockSpec((1, CHUNK, TILE, TILE), block)] + [VMEM] * len(more),
            out_specs=[VMEM, VMEM],
        ),
        out_shape=[
            pltpu.VMEM((sections, TB, TB * TILE, TILE), jnp.bfloat16),
            jax.ShapeDtypeStruct((8, 128), jnp.int32),
        ],
        input_output_aliases={4: 0} if more else {},
        compiler_params=params(12),
        cost_estimate=pl.CostEstimate(flops=0, bytes_accessed=15 << 20, transcendentals=0),
        name="build",
    )(tile_rows, tile_cols, tile_count, pltpu.with_memory_space_constraint(tile_values, pltpu.HBM), *map(in_vmem, more[:1]), *more[1:])


def place_of():
    return lax.axis_index("rep"), lax.rem(lax.axis_index("row"), 2)


def with_panels(kernel, name, panels, operands, outs, mib, flops=0):
    result = pl.pallas_call(
        kernel,
        in_specs=[VMEM] * (1 + len(operands)),
        out_specs=[VMEM] * (1 + len(outs)),
        out_shape=[pltpu.VMEM(panels.shape, panels.dtype), *outs],
        input_output_aliases={0: 0},
        compiler_params=params(mib),
        cost_estimate=pl.CostEstimate(flops=flops, bytes_accessed=2 << 20, transcendentals=0),
        name=name,
    )(in_vmem(panels), *operands)
    return result[0], result[1:]


def wide(panels, part, rows, at, size):
    return jnp.concatenate([panels[part, at + b, rows, :] for b in range(size)], axis=1)


def first_kernel(share, panels, source, token, same, out):
    replica, _ = place_of()
    for d in range(out.shape[0]):
        q = lax.rem(replica + d, out.shape[0])
        rows = pl.ds(pl.multiple_of(q * share, share), share)
        out[d] = jnp.dot(wide(panels, 0, rows, 0, TB), source[...], preferred_element_type=jnp.float32)


def second_kernel(share, shares, ds, panels, carried, inner, other, same, *outs):
    replica, core = place_of()
    source = jnp.where(core == 1, inner[...], other[...])
    for d, out in zip(ds, outs):
        q = lax.rem(replica + d, shares)
        rows = pl.ds(pl.multiple_of(q * share, share), share)
        total = carried[d] + jnp.dot(wide(panels, 1, rows, 0, TB), source, preferred_element_type=jnp.float32)
        out[...] = total.astype(out.dtype)


def sum_kernel(panels, *refs):
    parts, (same, out) = refs[:-2], refs[-2:]
    total = parts[0][...].astype(jnp.float32)
    for part in parts[1:]:
        total += part[...].astype(jnp.float32)
    out[...] = total


def middle_kernel(shares, count, panels, *refs):
    parts = refs[:count]
    weight, upstream, train_mask, same, activated, back, term, *sends = refs[count:]
    replica, _ = place_of()
    total = parts[0][...].astype(jnp.float32)
    for part in parts[1:]:
        total += part[...].astype(jnp.float32)
    aggregate = total.astype(jnp.bfloat16)
    logits = jnp.dot(aggregate, weight[...], preferred_element_type=jnp.float32)
    sigmoid_part = jax.nn.sigmoid(logits)
    activated[...] = (logits * sigmoid_part).astype(jnp.bfloat16)
    slope = sigmoid_part * (1.0 + logits * (1.0 - sigmoid_part))
    trained = jnp.broadcast_to(train_mask[...].astype(jnp.float32), logits.shape[::-1]).T
    masked = (upstream[...].astype(jnp.float32) * trained * slope).astype(jnp.bfloat16)
    turned = lax.dot_general(weight[...], masked, NT, preferred_element_type=jnp.float32).astype(jnp.bfloat16)
    back[...] = turned
    term[...] = lax.dot_general(aggregate, masked, TN, preferred_element_type=jnp.float32)
    width = weight.shape[0]
    some = width // shares
    for d, send in enumerate(sends, 1):
        at = pl.multiple_of(lax.rem(replica + d, shares) * some, some)
        send[:width, :] = turned
        send[width:, :] = term[pl.ds(at, some), :].astype(jnp.bfloat16)


def product_of(panels, part, q, es, backs, shares):
    replica, _ = place_of()
    width = share = backs[0].shape[1]
    total = None
    for e, back in zip(es, backs):
        p = lax.rem(replica + shares - e, shares)
        rows = pl.ds(pl.multiple_of(p * share, share), share)
        product = jnp.dot(back[:width, :], wide(panels, part, rows, 2 * q, 2), preferred_element_type=jnp.float32)
        total = product if total is None else total + product
    return total


def heads_kernel(shares, es, panels, *refs):
    backs = refs[: len(es)]
    same, late, early = refs[len(es) :]
    for part, out in ((1, late), (0, early)):
        for q in range(shares):
            out[q] = product_of(panels, part, q, es, backs, shares)


def tails_kernel(part, shares, es, qs, panels, carried, *refs):
    backs = refs[: len(es)]
    same, out = refs[len(es) :]
    for n, q in enumerate(qs):
        out[n] = (carried[q] + product_of(panels, part, q, es, backs, shares)).astype(out.dtype)


def tails_strip_kernel(part, shares, es, qs, panels, carried, *refs):
    backs, (term, *pieces) = refs[: len(es)], refs[len(es) : len(es) + 4]
    same, out, strips = refs[len(es) + 4 :]
    tails_kernel(part, shares, es, qs, panels, carried, *backs, same, out)
    replica, _ = place_of()
    width = term.shape[0]
    some = width // shares
    total = term[pl.ds(pl.multiple_of(replica * some, some), some), :]
    for piece in [*pieces, *backs]:
        total += piece[width:, :].astype(jnp.float32)
    for n in range(strips.shape[0]):
        strips[n] = total.astype(strips.dtype)


def merge_kernel(own, first, second, strips, *outs):
    replica, _ = place_of()
    half, width, _ = first.shape
    strip = strips[0].astype(jnp.float32)
    for n in range(1, strips.shape[0]):
        strip += strips[n].astype(jnp.float32)
    strip = strip.astype(jnp.bfloat16)
    for d, out in enumerate(outs):
        q = lax.rem(replica + d, len(outs))
        n = lax.rem(q, half)
        late = jnp.where(q < half, first[n], second[n])
        out[:width, :] = (own[q] + late.astype(jnp.float32)).astype(out.dtype)
        out[width:, :] = strip


def merge(own, first, second, strips):
    shares, width, share = own.shape
    return pl.pallas_call(
        merge_kernel,
        in_specs=[VMEM] * 4,
        out_specs=[VMEM] * shares,
        out_shape=[jax.ShapeDtypeStruct((width + strips.shape[1], share), jnp.bfloat16)] * shares,
        compiler_params=params(12),
        name="merge",
    )(own, first, second, strips)


def finish_kernel(scale, *refs):
    got, (home, whole) = refs[:-2], refs[-2:]
    replica, _ = place_of()
    width = whole.shape[0]
    some = width // len(got)
    total = got[0][:width, :].astype(jnp.float32)
    for part in got[1:]:
        total += part[:width, :].astype(jnp.float32)
    home[...] = total.T.astype(home.dtype)
    for d, part in enumerate(got):
        at = pl.multiple_of(lax.rem(replica + len(got) - d, len(got)) * some, some)
        whole[pl.ds(at, some), :] = part[width:, :].astype(jnp.float32) * scale


def finish(scale, width, got):
    share = got[0].shape[1]
    return pl.pallas_call(
        functools.partial(finish_kernel, scale),
        in_specs=[VMEM] * len(got),
        out_specs=[VMEM, VMEM],
        out_shape=[
            jax.ShapeDtypeStruct((share, width), jnp.bfloat16),
            jax.ShapeDtypeStruct((width, share), jnp.float32),
        ],
        compiler_params=params(12),
        name="finish",
    )(*got)


def pairs(row_devices, rep_devices, target):
    found = []
    for i in range(row_devices):
        for r in range(rep_devices):
            j, q = target(i, r)
            found.append((i * rep_devices + r, (j % row_devices) * rep_devices + q % rep_devices))
    return found


MAIN_FROM = (0, 5, 2, 7, 4, 1, 6, 3)
OTHER_FROM = (1, 6, 3, 0, 5, 2, 7, 4)


def per_device(features, weight, tile_values, tile_rows, tile_cols, tile_count, train_mask, upstream):
    rows_n, reps = lax.axis_size("row"), lax.axis_size("rep")
    sections = rows_n // reps
    width = weight.shape[0]
    share = features.shape[0] // reps
    bf16, f32 = jnp.bfloat16, jnp.float32

    def moved(value, target):
        return lax.ppermute(value, ("row", "rep"), pairs(rows_n, reps, target))

    def fetched(value, back, sources, wanted=lambda i: True):
        found = [
            (((i - sections * r - back) % rows_n) * reps + sources[r], i * reps + r)
            for i in range(rows_n)
            for r in range(reps)
            if wanted(i)
        ]
        return lax.ppermute(value, ("row", "rep"), found)

    def to_other_core(value):
        return lax.ppermute(value, ("row", "rep"), [((i - 1) * reps + r, i * reps + r) for i in range(1, rows_n, 2) for r in range(reps)])

    main = fetched(features, 0, MAIN_FROM)
    lists = tile_values[0, 0], tile_rows[0, 0], tile_cols[0, 0], tile_count[0, 0]
    panels, token = build(0, *lists)
    held, token = lax.optimization_barrier((features, token))
    other = fetched(held, 1, OTHER_FROM, lambda i: i % 2 == 0)
    panels, token = build(1, *lists, panels, token)
    main, token = lax.optimization_barrier((main, token))
    inner = to_other_core(main)

    flops = features.shape[0] ** 2 * 2 * width
    panels, (carried,) = with_panels(
        functools.partial(first_kernel, share), "first", panels, [main, token],
        [jax.ShapeDtypeStruct((reps, share, width), f32)], 12, flops,
    )
    shares_out = {}
    for ds in ((1, 2, 3, 4), (5, 6, 7, 0)):
        panels, outs = with_panels(
            functools.partial(second_kernel, share, reps, ds), "second", panels, [carried, inner, other],
            [jax.ShapeDtypeStruct((share, width), bf16)] * len(ds), 12, flops // 2,
        )
        shares_out.update(zip(ds, outs))
    received = [shares_out[0]] + [moved(shares_out[d], lambda i, r, d=d: (i, r + d)) for d in range(1, reps)]
    half = reps // 2 + 1
    panels, (some,) = with_panels(sum_kernel, "some", panels, received[1:half], [jax.ShapeDtypeStruct((share, width), f32)], 12)
    received = [some, shares_out[0], *received[half:]]

    panels, results = with_panels(
        functools.partial(middle_kernel, reps, len(received)), "middle", panels, [*received, weight, upstream, train_mask.reshape(1, share)],
        [
            jax.ShapeDtypeStruct((share, width), bf16),
            jax.ShapeDtypeStruct((width, share), bf16),
            jax.ShapeDtypeStruct((width, width), f32),
        ]
        + [jax.ShapeDtypeStruct((width + width // reps, share), bf16)] * (reps - 1),
        12,
    )
    activated, back, term, *sends = results
    backs = [back] + [moved(send, lambda i, r, d=d: (i, r + d)) for d, send in enumerate(sends, 1)]

    shares = tuple(range(reps))
    head, tail = shares[:4], shares[4:]
    halves = shares[: reps // 2], shares[reps // 2 :]
    sums = jax.ShapeDtypeStruct((reps, width, share), f32)
    panels, (late_sum, early_sum) = with_panels(
        functools.partial(heads_kernel, reps, head), "heads", panels, backs[:4], [sums, sums], 12, flops
    )
    piece_out = pltpu.VMEM((reps // 2, width, share), bf16)
    strip_out = jax.ShapeDtypeStruct((rows_n // 2, width // reps, width), bf16)
    panels, (piece, strips) = with_panels(
        functools.partial(tails_strip_kernel, 1, reps, tail, halves[0]), "late_strip", panels,
        [late_sum, *backs[4:], term, *backs[1:4]], [piece_out, strip_out], 12, flops // 4,
    )
    first = moved(piece, lambda i, r: (i - 1, r) if i % 2 else (i + 1, r + 1))
    panels, (piece,) = with_panels(
        functools.partial(tails_kernel, 1, reps, tail, halves[1]), "late", panels, [late_sum, *backs[4:]], [piece_out], 12, flops // 4
    )
    second = moved(piece, lambda i, r: (i - 1, r))
    panels, (own,) = with_panels(
        functools.partial(tails_kernel, 0, reps, tail, shares), "early", panels, [early_sum, *backs[4:]], [sums], 12, flops // 2
    )
    strips, own = lax.optimization_barrier((strips, own))
    same_core = [[i * reps + r for i in range(c, rows_n, 2)] for c in range(2) for r in range(reps)]
    strips = lax.all_to_all(strips + moved(strips, lambda i, r: (i ^ 1, r)), ("row", "rep"), 0, 0, axis_index_groups=same_core)

    merged = merge(own, first, second, strips)
    got = [moved(merged[d], lambda i, r, d=d: (i - sections * r, r + d)) for d in shares]
    feature_grad, whole = finish(1.0 / math.sqrt(features.shape[0] * rows_n), width, got)
    return activated, whole, feature_grad


def solution(mesh):
    placed = (
        P("row", None),
        P(),
        P("row", "rep", None, None, None, None),
        P("row", "rep", None, None),
        P("row", "rep", None, None),
        P("row", "rep", None),
        P(("row", "rep")),
        P(("row", "rep"), None),
    )
    return jax.shard_map(
        per_device,
        mesh=mesh,
        in_specs=placed,
        out_specs=(P(("row", "rep"), None), P(), P(("row", "rep"), None)),
        check_vma=False,
    )
```

```python
import functools
import math

import jax
import jax.numpy as jnp
from jax import lax
from jax.experimental import pallas as pl
from jax.experimental.pallas import tpu as pltpu
from jax.sharding import PartitionSpec as P

TB = 16
TILE = 128
CHUNK = 48
VMEM = pl.BlockSpec(memory_space=pltpu.VMEM)
SMEM = pl.BlockSpec(memory_space=pltpu.SMEM)
NT = (((1,), (1,)), ((), ()))
TN = (((0,), (0,)), ((), ()))


def params(mib, **more):
    return pltpu.CompilerParams(vmem_limit_bytes=mib << 20, **more)


def in_vmem(array):
    return pltpu.with_memory_space_constraint(array, pltpu.VMEM)


def build_kernel(part, rows, cols, count, tiles, *refs):
    panels, token = refs[-2:]
    chunk = pl.program_id(0)
    token[...] = jnp.zeros(token.shape, token.dtype)

    @pl.when(chunk == 0)
    def _():
        def clear(b, carry):
            panels[part, b] = jnp.zeros(panels.shape[2:], panels.dtype)
            return carry

        lax.fori_loop(0, TB, clear, 0)

    def place(t, carry):
        slot = chunk * CHUNK + t
        row = pl.multiple_of(rows[part, slot] * TILE, TILE)
        panels[part, cols[part, slot], pl.ds(row, TILE), :] = tiles[0, t]
        return carry

    lax.fori_loop(0, jnp.clip(count[part] - chunk * CHUNK, 0, CHUNK), place, 0)


def build(part, tile_values, tile_rows, tile_cols, tile_count, *more):
    sections, slots = tile_rows.shape

    def block(chunk, rows, cols, count):
        last = lax.div(count[part] - 1, CHUNK)
        return part, jnp.minimum(chunk, last), 0, 0

    return pl.pallas_call(
        functools.partial(build_kernel, part),
        grid_spec=pltpu.PrefetchScalarGridSpec(
            num_scalar_prefetch=3,
            grid=(slots // CHUNK,),
            in_specs=[pl.BlockSpec((1, CHUNK, TILE, TILE), block)] + [VMEM] * len(more),
            out_specs=[VMEM, VMEM],
        ),
        out_shape=[
            pltpu.VMEM((sections, TB, TB * TILE, TILE), jnp.bfloat16),
            jax.ShapeDtypeStruct((8, 128), jnp.int32),
        ],
        input_output_aliases={4: 0} if more else {},
        compiler_params=params(12),
        cost_estimate=pl.CostEstimate(flops=0, bytes_accessed=15 << 20, transcendentals=0),
        name="build",
    )(tile_rows, tile_cols, tile_count, pltpu.with_memory_space_constraint(tile_values, pltpu.HBM), *map(in_vmem, more[:1]), *more[1:])


def place_of():
    return lax.axis_index("rep"), lax.rem(lax.axis_index("row"), 2)


def with_panels(kernel, name, panels, operands, outs, mib, flops=0):
    result = pl.pallas_call(
        kernel,
        in_specs=[VMEM] * (1 + len(operands)),
        out_specs=[VMEM] * (1 + len(outs)),
        out_shape=[pltpu.VMEM(panels.shape, panels.dtype), *outs],
        input_output_aliases={0: 0},
        compiler_params=params(mib),
        cost_estimate=pl.CostEstimate(flops=flops, bytes_accessed=2 << 20, transcendentals=0),
        name=name,
    )(in_vmem(panels), *operands)
    return result[0], result[1:]


def wide(panels, part, rows, at, size):
    return jnp.concatenate([panels[part, at + b, rows, :] for b in range(size)], axis=1)


def first_kernel(share, panels, source, token, same, out):
    replica, _ = place_of()
    for d in range(out.shape[0]):
        q = lax.rem(replica + d, out.shape[0])
        rows = pl.ds(pl.multiple_of(q * share, share), share)
        out[d] = jnp.dot(wide(panels, 0, rows, 0, TB), source[...], preferred_element_type=jnp.float32)


def second_kernel(share, shares, ds, panels, carried, inner, other, same, *outs):
    replica, core = place_of()
    source = jnp.where(core == 1, inner[...], other[...])
    for d, out in zip(ds, outs):
        q = lax.rem(replica + d, shares)
        rows = pl.ds(pl.multiple_of(q * share, share), share)
        total = carried[d] + jnp.dot(wide(panels, 1, rows, 0, TB), source, preferred_element_type=jnp.float32)
        out[...] = total.astype(out.dtype)


def sum_kernel(panels, *refs):
    parts, (same, out) = refs[:-2], refs[-2:]
    total = parts[0][...].astype(jnp.float32)
    for part in parts[1:]:
        total += part[...].astype(jnp.float32)
    out[...] = total


def middle_kernel(shares, count, panels, *refs):
    parts = refs[:count]
    weight, upstream, train_mask, same, activated, back, term, *sends = refs[count:]
    replica, _ = place_of()
    total = parts[0][...].astype(jnp.float32)
    for part in parts[1:]:
        total += part[...].astype(jnp.float32)
    aggregate = total.astype(jnp.bfloat16)
    logits = jnp.dot(aggregate, weight[...], preferred_element_type=jnp.float32)
    sigmoid_part = jax.nn.sigmoid(logits)
    activated[...] = (logits * sigmoid_part).astype(jnp.bfloat16)
    slope = sigmoid_part * (1.0 + logits * (1.0 - sigmoid_part))
    trained = jnp.broadcast_to(train_mask[...].astype(jnp.float32), logits.shape[::-1]).T
    masked = (upstream[...].astype(jnp.float32) * trained * slope).astype(jnp.bfloat16)
    turned = lax.dot_general(weight[...], masked, NT, preferred_element_type=jnp.float32).astype(jnp.bfloat16)
    back[...] = turned
    term[...] = lax.dot_general(aggregate, masked, TN, preferred_element_type=jnp.float32)
    width = weight.shape[0]
    some = width // shares
    for d, send in enumerate(sends, 1):
        at = pl.multiple_of(lax.rem(replica + d, shares) * some, some)
        send[:width, :] = turned
        send[width:, :] = term[pl.ds(at, some), :].astype(jnp.bfloat16)


def product_of(panels, part, q, es, backs, shares):
    replica, _ = place_of()
    width = share = backs[0].shape[1]
    total = None
    for e, back in zip(es, backs):
        p = lax.rem(replica + shares - e, shares)
        rows = pl.ds(pl.multiple_of(p * share, share), share)
        product = jnp.dot(back[:width, :], wide(panels, part, rows, 2 * q, 2), preferred_element_type=jnp.float32)
        total = product if total is None else total + product
    return total


def heads_kernel(shares, es, panels, *refs):
    backs = refs[: len(es)]
    same, late, early = refs[len(es) :]
    for part, out in ((1, late), (0, early)):
        for q in range(shares):
            out[q] = product_of(panels, part, q, es, backs, shares)


def tails_kernel(part, shares, es, qs, panels, carried, *refs):
    backs = refs[: len(es)]
    same, out = refs[len(es) :]
    for n, q in enumerate(qs):
        out[n] = (carried[q] + product_of(panels, part, q, es, backs, shares)).astype(out.dtype)


def tails_strip_kernel(part, shares, es, qs, panels, carried, *refs):
    backs, (term, *pieces) = refs[: len(es)], refs[len(es) : len(es) + 4]
    same, out, strips = refs[len(es) + 4 :]
    tails_kernel(part, shares, es, qs, panels, carried, *backs, same, out)
    replica, _ = place_of()
    width = term.shape[0]
    some = width // shares
    total = term[pl.ds(pl.multiple_of(replica * some, some), some), :]
    for piece in [*pieces, *backs]:
        total += piece[width:, :].astype(jnp.float32)
    for n in range(strips.shape[0]):
        strips[n] = total.astype(strips.dtype)


def merge_kernel(own, first, second, strips, *outs):
    replica, _ = place_of()
    half, width, _ = first.shape
    strip = strips[0].astype(jnp.float32)
    for n in range(1, strips.shape[0]):
        strip += strips[n].astype(jnp.float32)
    strip = strip.astype(jnp.bfloat16)
    for d, out in enumerate(outs):
        q = lax.rem(replica + d, len(outs))
        n = lax.rem(q, half)
        late = jnp.where(q < half, first[n], second[n])
        out[:width, :] = (own[q] + late.astype(jnp.float32)).astype(out.dtype)
        out[width:, :] = strip


def merge(own, first, second, strips):
    shares, width, share = own.shape
    return pl.pallas_call(
        merge_kernel,
        in_specs=[VMEM] * 4,
        out_specs=[VMEM] * shares,
        out_shape=[jax.ShapeDtypeStruct((width + strips.shape[1], share), jnp.bfloat16)] * shares,
        compiler_params=params(12),
        name="merge",
    )(own, first, second, strips)


def finish_kernel(scale, order, *refs):
    got, (home, whole) = refs[:-2], refs[-2:]
    replica, _ = place_of()
    width = whole.shape[0]
    some = width // len(got)
    total = got[0][:width, :].astype(jnp.float32)
    for part in got[1:]:
        total += part[:width, :].astype(jnp.float32)
    home[...] = total.T.astype(home.dtype)
    for d, part in zip(order, got):
        at = pl.multiple_of(lax.rem(replica + len(got) - d, len(got)) * some, some)
        whole[pl.ds(at, some), :] = part[width:, :].astype(jnp.float32) * scale


def finish(scale, width, order, got):
    share = got[0].shape[1]
    return pl.pallas_call(
        functools.partial(finish_kernel, scale, order),
        in_specs=[VMEM] * len(got),
        out_specs=[VMEM, VMEM],
        out_shape=[
            jax.ShapeDtypeStruct((share, width), jnp.bfloat16),
            jax.ShapeDtypeStruct((width, share), jnp.float32),
        ],
        compiler_params=params(12),
        name="finish",
    )(*got)


def pairs(row_devices, rep_devices, target):
    found = []
    for i in range(row_devices):
        for r in range(rep_devices):
            j, q = target(i, r)
            found.append((i * rep_devices + r, (j % row_devices) * rep_devices + q % rep_devices))
    return found


MAIN_FROM = (0, 5, 2, 7, 4, 1, 6, 3)
OTHER_FROM = (1, 6, 3, 0, 5, 2, 7, 4)


def per_device(features, weight, tile_values, tile_rows, tile_cols, tile_count, train_mask, upstream):
    rows_n, reps = lax.axis_size("row"), lax.axis_size("rep")
    sections = rows_n // reps
    width = weight.shape[0]
    share = features.shape[0] // reps
    bf16, f32 = jnp.bfloat16, jnp.float32

    def moved(value, target):
        return lax.ppermute(value, ("row", "rep"), pairs(rows_n, reps, target))

    def fetched(value, back, sources, wanted=lambda i: True):
        found = [
            (((i - sections * r - back) % rows_n) * reps + sources[r], i * reps + r)
            for i in range(rows_n)
            for r in range(reps)
            if wanted(i)
        ]
        return lax.ppermute(value, ("row", "rep"), found)

    def to_other_core(value):
        return lax.ppermute(value, ("row", "rep"), [((i - 1) * reps + r, i * reps + r) for i in range(1, rows_n, 2) for r in range(reps)])

    main = fetched(features, 0, MAIN_FROM)
    lists = tile_values[0, 0], tile_rows[0, 0], tile_cols[0, 0], tile_count[0, 0]
    panels, token = build(0, *lists)
    held, token = lax.optimization_barrier((features, token))
    other = fetched(held, 1, OTHER_FROM, lambda i: i % 2 == 0)
    panels, token = build(1, *lists, panels, token)
    main, token = lax.optimization_barrier((main, token))
    inner = to_other_core(main)

    flops = features.shape[0] ** 2 * 2 * width
    panels, (carried,) = with_panels(
        functools.partial(first_kernel, share), "first", panels, [main, token],
        [jax.ShapeDtypeStruct((reps, share, width), f32)], 12, flops,
    )
    shares_out = {}
    for ds in ((1, 2, 3, 4), (5, 6, 7, 0)):
        panels, outs = with_panels(
            functools.partial(second_kernel, share, reps, ds), "second", panels, [carried, inner, other],
            [jax.ShapeDtypeStruct((share, width), bf16)] * len(ds), 12, flops // 2,
        )
        shares_out.update(zip(ds, outs))
    received = [shares_out[0]] + [moved(shares_out[d], lambda i, r, d=d: (i, r + d)) for d in range(1, reps)]
    half = reps // 2 + 1
    panels, (some,) = with_panels(sum_kernel, "some", panels, received[1:half], [jax.ShapeDtypeStruct((share, width), f32)], 12)
    received = [some, shares_out[0], *received[half:]]

    panels, results = with_panels(
        functools.partial(middle_kernel, reps, len(received)), "middle", panels, [*received, weight, upstream, train_mask.reshape(1, share)],
        [
            jax.ShapeDtypeStruct((share, width), bf16),
            jax.ShapeDtypeStruct((width, share), bf16),
            jax.ShapeDtypeStruct((width, width), f32),
        ]
        + [jax.ShapeDtypeStruct((width + width // reps, share), bf16)] * (reps - 1),
        12,
    )
    activated, back, term, *sends = results
    backs = [back] + [moved(send, lambda i, r, d=d: (i, r + d)) for d, send in enumerate(sends, 1)]

    shares = tuple(range(reps))
    head, tail = shares[:4], shares[4:]
    halves = shares[: reps // 2], shares[reps // 2 :]
    sums = jax.ShapeDtypeStruct((reps, width, share), f32)
    panels, (late_sum, early_sum) = with_panels(
        functools.partial(heads_kernel, reps, head), "heads", panels, backs[:4], [sums, sums], 12, flops
    )
    piece_out = pltpu.VMEM((reps // 2, width, share), bf16)
    strip_out = jax.ShapeDtypeStruct((rows_n // 2, width // reps, width), bf16)
    panels, (piece, strips) = with_panels(
        functools.partial(tails_strip_kernel, 1, reps, tail, halves[0]), "late_strip", panels,
        [late_sum, *backs[4:], term, *backs[1:4]], [piece_out, strip_out], 12, flops // 4,
    )
    first = moved(piece, lambda i, r: (i - 1, r) if i % 2 else (i + 1, r + 1))
    panels, (piece,) = with_panels(
        functools.partial(tails_kernel, 1, reps, tail, halves[1]), "late", panels, [late_sum, *backs[4:]], [piece_out], 12, flops // 4
    )
    second = moved(piece, lambda i, r: (i - 1, r))
    panels, (own,) = with_panels(
        functools.partial(tails_kernel, 0, reps, tail, shares), "early", panels, [early_sum, *backs[4:]], [sums], 12, flops // 2
    )
    strips, own = lax.optimization_barrier((strips, own))
    same_core = [[i * reps + r for i in range(c, rows_n, 2)] for c in range(2) for r in range(reps)]
    strips = lax.all_to_all(strips + moved(strips, lambda i, r: (i ^ 1, r)), ("row", "rep"), 0, 0, axis_index_groups=same_core)

    merged = merge(own, first, second, strips)
    order = (7, 6, 5, 4, 3, 2, 1, 0)
    found = {d: moved(merged[d], lambda i, r, d=d: (i - sections * r, r + d)) for d in order}
    feature_grad, whole = finish(1.0 / math.sqrt(features.shape[0] * rows_n), width, order, [found[d] for d in order])
    return activated, whole, feature_grad


def solution(mesh):
    placed = (
        P("row", None),
        P(),
        P("row", "rep", None, None, None, None),
        P("row", "rep", None, None),
        P("row", "rep", None, None),
        P("row", "rep", None),
        P(("row", "rep")),
        P(("row", "rep"), None),
    )
    return jax.shard_map(
        per_device,
        mesh=mesh,
        in_specs=placed,
        out_specs=(P(("row", "rep"), None), P(), P(("row", "rep"), None)),
        check_vma=False,
    )
```
